128 devices in a mesh: dp: 128 (over y, x, z, core).
Axes of the slice: x: 4, y: 4, z: 4, core: 2. Of those that a mesh axis runs over, the one named last changes fastest.
Arguments:
- tokens: bfloat16 [73728, 2048], P('dp'), may hold values from -24 to 24
- route_gate: bfloat16 [73728], P('dp'), may hold values from 0.049804688 to 1
- cotangent: bfloat16 [73728, 2048], P('dp'), may hold values from -6 to 6
- row_count: int32 [128], P('dp'), may hold values from 1 to 576, 24576 in all
- w_gate: bfloat16 [2048, 1024], P('dp'), may hold values from -0.125 to 0.125
- w_up: bfloat16 [2048, 1024], P('dp'), may hold values from -0.125 to 0.125
- w_down: bfloat16 [2048, 1024], P('dp'), may hold values from -0.1875 to 0.1875
Outputs:
- mixed: bfloat16 [73728, 2048], P('dp')
- token_grad: bfloat16 [73728, 2048], P('dp')
- grad_gate: float32 [2048, 1024], P('dp')
- grad_up: float32 [2048, 1024], P('dp')
- grad_down: float32 [2048, 1024], P('dp')
The draws below stay inside these ranges and needn't reach their ends.
Inputs may be any that keep to these rules, and one draw needn't show every extreme that they name: row_count sums to 192 * the number of devices; rows beyond a device's count are not part of its micro-batch.
All inputs are finite; a program needn't handle non-finite values.
Results may differ from the reference program's by a relative error of at most 0.0057.
Values may be sent and summed in bfloat16 or wider, within the bound.
A program may use at most 192 MiB of HBM per device.

```python
import math
import jax
import jax.numpy as jnp
import numpy as np
from jax import lax

D = 2048
FF = 1024
ROWS_MEAN = 192
TOKENS = 73728
N_DP = 128


def spiked(values, key, source, target, shards_of, factor):
    owner, partner = [(jnp.arange(values.shape[position]) // (values.shape[position] // shards_of)).reshape([-1 if axis == position else 1 for axis in range(values.ndim)]) for position in (source, target)]
    chosen = jax.random.permutation(key, shards_of)[partner]
    strong = (owner == chosen) | (owner == (partner + shards_of // 2) % shards_of)
    return jnp.where(strong, factor * values, values)


def levels(key, shape, split, low, largest):
    loudness, own = 1.0, jax.random.fold_in(key, 6)
    for dim, parts in split:
        heights = jnp.exp(jax.random.uniform(jax.random.fold_in(own, dim), (parts,), jnp.float32, low / len(split), largest / len(split)))
        loudness = loudness * jnp.repeat(heights, shape[dim] // parts).reshape([-1 if axis == dim else 1 for axis in range(len(shape))])
    return loudness


def length_profile(count, total, limit, slope):
    portions = [(1 << 20) // math.isqrt(rank ** slope) + 1 for rank in range(2, count + 1)]
    rest, given = total - limit - (count - 1), [1] * (count - 1)
    while rest > 0:
        candidates = [i for i in range(count - 1) if given[i] < limit]
        pool, budget = sum([portions[i] for i in candidates]), rest
        for i in candidates:
            addition = min(limit - given[i], max(1, budget * portions[i] // pool), rest)
            given[i] = given[i] + addition
            rest = rest - addition
    return np.array([limit] + given)


def uneven(stream_key, number_of, total, most, skew):
    if number_of == 2:
        one = jax.random.randint(stream_key, (), max(1, total - most), min(most, total - 1) + 1)
        return jnp.stack([one, total - one])
    lengths = jnp.asarray(length_profile(number_of, total, most, skew), jnp.int32)
    pairs = (number_of - 1) // 2
    giver, taker = lengths[1:1 + 2 * pairs:2], lengths[2:2 + 2 * pairs:2]
    slack = jnp.minimum(giver - 1, most - taker)
    shifted = jax.random.randint(jax.random.fold_in(stream_key, 1), (pairs,), 0, 1 << 20) % (slack + 1)
    lengths = lengths.at[1:1 + 2 * pairs:2].set(giver - shifted).at[2:2 + 2 * pairs:2].set(taker + shifted)
    return lengths[jax.random.permutation(jax.random.fold_in(stream_key, 2), number_of)]


def bell_draw(stream_key, extent, spread, reach, cuts=(), held_as=jnp.bfloat16):
    level = levels(stream_key, extent, cuts, -0.22, 0.18) if cuts else 1.0
    values = jax.random.normal(stream_key, extent, jnp.float32) * spread * level
    return jnp.minimum(jnp.maximum(values, -reach), reach).astype(held_as)


def gaussian_with(own_key, extent, scale, reach, shards, heavy, kind=jnp.bfloat16):
    entries = scale * jax.random.normal(own_key, extent, jnp.float32)
    if shards:
        entries = entries * levels(own_key, extent, shards, -0.22, 0.18)
    return jnp.clip(spiked(entries, jax.random.fold_in(own_key, 3), *heavy), -reach, reach).astype(kind)


def setup_inputs(seed: int = 0) -> dict:
    keys = jax.random.split(jax.random.key(seed), 8)
    tokens = gaussian_with(keys[0], (TOKENS, D), 1.0, 24.0, ((0, 128),), (0, 1, 128, 5.5))
    route_gate = jnp.clip(jnp.exp(math.log(1.0) - 2.9996462 * jax.random.uniform(keys[1], (TOKENS,), jnp.float32) ** levels(keys[1], (TOKENS,), ((0, 128),), -0.2, 0.2)), 0.049804688, 1.0).astype(jnp.bfloat16)
    cotangent = bell_draw(keys[2], (TOKENS, D), 1.0, 6.0, ((0, 128),))
    row_count = uneven(keys[3], N_DP, ROWS_MEAN * N_DP, 3 * ROWS_MEAN, 2).astype(jnp.int32)
    w_gate = bell_draw(keys[4], (D, FF), D ** -0.5, 0.125, ((0, 128),))
    w_up = bell_draw(keys[5], (D, FF), D ** -0.5, 0.125, ((0, 128),))
    w_down = bell_draw(keys[6], (D, FF), FF ** -0.5, 0.1875, ((0, 128),))
    return dict(tokens=tokens, route_gate=route_gate, cotangent=cotangent, row_count=row_count, w_gate=w_gate, w_up=w_up, w_down=w_down)


def contract_rows(left_part, right_part):
    return lax.dot_general(left_part, right_part, (((0,), (0,)), ((), ())), preferred_element_type=jnp.float32)


def contract_cols(left_part, right_part):
    return lax.dot_general(left_part, right_part, (((1,), (1,)), ((), ())), preferred_element_type=jnp.float32)


def expert_rows(rows_in, row_gain, cot_rows, gate_full, up_full, down_full):
    gain_col = row_gain.astype(jnp.float32)[:, None]
    gate_pre = jnp.dot(rows_in, gate_full, preferred_element_type=jnp.float32)
    up_pre = jnp.dot(rows_in, up_full, preferred_element_type=jnp.float32)
    sigma_gate = jax.nn.sigmoid(gate_pre)
    silu_gate = gate_pre * sigma_gate
    hidden = (silu_gate * up_pre).astype(jnp.bfloat16)
    projected = contract_cols(hidden, down_full)
    mixed = (gain_col * projected).astype(jnp.bfloat16)
    out_grad = (gain_col * cot_rows.astype(jnp.float32)).astype(jnp.bfloat16)
    act_grad = jnp.dot(out_grad, down_full, preferred_element_type=jnp.float32)
    gate_grad = (act_grad * up_pre * sigma_gate * (1.0 + gate_pre * (1.0 - sigma_gate))).astype(jnp.bfloat16)
    up_grad = (act_grad * silu_gate).astype(jnp.bfloat16)
    token_grad = (contract_cols(gate_grad, gate_full) + contract_cols(up_grad, up_full)).astype(jnp.bfloat16)
    return mixed, token_grad, gate_grad, up_grad, out_grad, hidden


def reference(tokens, route_gate, cotangent, row_count, w_gate, w_up, w_down):
    row_slots = tokens.shape[0] // N_DP
    live_row = (jnp.arange(row_slots, dtype=jnp.int32)[None, :] < row_count[:, None]).reshape(-1)
    picked = jnp.nonzero(live_row, size=ROWS_MEAN * N_DP)[0].astype(jnp.int32)
    rows_in = tokens[picked]
    mixed_rows, grad_rows, gate_grad, up_grad, out_grad, hidden = expert_rows(
        rows_in, route_gate[picked], cotangent[picked], w_gate, w_up, w_down)
    mixed = jnp.zeros_like(tokens).at[picked].set(mixed_rows)
    token_grad = jnp.zeros_like(tokens).at[picked].set(grad_rows)
    grad_gate = contract_rows(rows_in, gate_grad)
    grad_up = contract_rows(rows_in, up_grad)
    grad_down = contract_rows(out_grad, hidden)
    return mixed, token_grad, grad_gate, grad_up, grad_down
```

```python
import functools

import jax
import jax.numpy as jnp
from jax import lax
from jax.experimental import pallas as pl
from jax.experimental.pallas import tpu as pltpu
from jax.sharding import PartitionSpec as P

bf16 = jnp.bfloat16
f32 = jnp.float32
H = 2
NT = (((1,), (1,)), ((), ()))
ORDER = ((32, 4, 1), (1, 32, 4), (4, 1, 32))


def place(p, d):
    y, x, z, core = d // 32, d // 8 % 4, d // 2 % 4, d % 2
    k = y * ORDER[p][0] + x * ORDER[p][1] + z * ORDER[p][2]
    return 16 * (k // 32 * 32 + core * 16 + k % 32)


def stride(p):
    return 32 - 33 * p + 9 * p * p


def al(v, n=16):
    return pl.multiple_of(v, n)


def kernel(
    tok_in, cot_in, gain_in, wg_in, wu_in, wd_in,
    mixed, tgrad, out_g, out_u, out_d,
    tok, og, gain, wt, lt, acc, gr, part, sd, rd, cr, br, ar,
    loc, ss, ra, rb, rc, rf, rdg, dS, dR, cS, cR, bS, bR, aS, aR,
):
    F = wt.shape[2]
    me = lax.axis_index("dp")
    core = me % 2
    sib = me + 1 - 2 * core

    def coord(p):
        return me // stride(p) % 4

    def dev(p, r):
        s = stride(p)
        k = me // s % 4
        return me + ((k + r) % 4 - k) * s

    def ax(p):
        return p, (p + 1) % 3, (p + 2) % 3

    def rcopy(src, dst, ssem, rsem, to):
        c = pltpu.make_async_remote_copy(
            src_ref=src, dst_ref=dst, send_sem=ssem, recv_sem=rsem,
            device_id=(to,), device_id_type=pl.DeviceIdType.MESH)
        c.start()

    def got(ref, sem):
        pltpu.make_async_copy(ref, ref, sem).wait()

    def each(fn):
        def step(p, _):
            fn(p)
            return 0
        lax.fori_loop(0, 3, step, 0)

    own = [me // 32 * wy + me // 8 % 4 * wx + me // 2 % 4 * wz for wy, wx, wz in ORDER]
    own = [al(16 * (k // 32 * 32 + core * 16 + k % 32)) for k in own]
    cps = []
    for h in range(H):
        for p, w in enumerate((wg_in, wu_in, wd_in)):
            cps.append(pltpu.make_async_copy(
                w.at[:, pl.ds(h * F, F)], wt.at[h * 3 + p, pl.ds(own[p], 16)], loc.at[h * 3 + p]))
    big = [pltpu.make_async_copy(tok_in, tok, loc.at[6]),
           pltpu.make_async_copy(cot_in, og, loc.at[7]),
           pltpu.make_async_copy(gain_in, gain, loc.at[8])]
    for c in cps + big:
        c.start()

    bar = pltpu.get_barrier_semaphore()
    for p in range(3):
        for r in (1, 2, 3):
            pl.semaphore_signal(bar, inc=1, device_id=(dev(p, r),), device_id_type=pl.DeviceIdType.MESH)
    pl.semaphore_signal(bar, inc=1, device_id=(sib,), device_id_type=pl.DeviceIdType.MESH)
    pl.semaphore_wait(bar, 10)
    for c in cps:
        c.wait()

    def base(p):
        sl, mi, fa = ax(p)
        return coord(sl), coord(mi), coord(fa)

    def ag_a(h):
        def fn(p):
            kc, kb, ka = base(p)
            hp = h * 3 + p
            blk = wt.at[hp, pl.ds(al(kc * 512 + core * 256 + kb * 64 + ka * 16), 16)]
            for r in (1, 2, 3):
                rcopy(blk, blk, ss.at[hp], ra.at[hp], dev(ax(p)[2], r))
        each(fn)

    def line(p, hp, kb):
        return wt.at[hp, pl.ds(al(coord(p) * 512 + core * 256 + kb * 64, 64), 64)]

    def send_line(p, hp, kb):
        ref = line(p, hp, kb)
        half = kb // 2
        rcopy(ref, ref, ss.at[hp], rc.at[hp * 4 + half], dev(p, 1))
        rcopy(ref, ref, ss.at[hp], rc.at[hp * 4 + 2 + half], dev(p, 3))

    def ag_b(h):
        def fn(p):
            hp = h * 3 + p
            kb = coord(ax(p)[1])
            got(wt.at[hp, pl.ds(0, 48)], ra.at[hp])
            ref = line(p, hp, kb)
            for r in (1, 2, 3):
                rcopy(ref, ref, ss.at[hp], rb.at[hp], dev(ax(p)[1], r))
            send_line(p, hp, kb)
        each(fn)

    def plane(hp, kc):
        return wt.at[hp, pl.ds(al(kc * 512 + core * 256, 256), 256)]

    def to_sib(p, hp, r):
        ref = plane(hp, (coord(p) + r) % 4)
        rcopy(ref, ref, ss.at[hp], rdg.at[hp * 4 + r], sib)

    def ag_c(h):
        def fn(p):
            hp = h * 3 + p
            kb = coord(ax(p)[1])
            got(wt.at[hp, pl.ds(0, 192)], rb.at[hp])
            for j in (1, 2, 3):
                send_line(p, hp, (kb + j) % 4)
            to_sib(p, hp, 0)
        each(fn)

    def ag_f(h):
        def fn(p):
            hp = h * 3 + p
            low = wt.at[hp, pl.ds(0, 128)]
            got(low, rc.at[hp * 4])
            src = wt.at[hp, pl.ds(al((coord(p) + 3) % 4 * 512 + core * 256, 256), 128)]
            rcopy(src, src, ss.at[hp], rf.at[hp * 2], dev(p, 1))
            got(low, rc.at[hp * 4 + 3])
            src = wt.at[hp, pl.ds(al((coord(p) + 1) % 4 * 512 + core * 256 + 128, 128), 128)]
            rcopy(src, src, ss.at[hp], rf.at[hp * 2 + 1], dev(p, 3))
            got(low, rc.at[hp * 4 + 1])
            to_sib(p, hp, 3)
            got(low, rc.at[hp * 4 + 2])
            to_sib(p, hp, 1)
        each(fn)

    def ag_g(h):
        def fn(p):
            hp = h * 3 + p
            got(wt.at[hp, pl.ds(0, 128)], rf.at[hp * 2])
            got(wt.at[hp, pl.ds(0, 128)], rf.at[hp * 2 + 1])
            to_sib(p, hp, 2)
        each(fn)

    def ag_wait(h, p):
        hp = h * 3 + p
        for r in range(4):
            got(plane(hp, r), rdg.at[hp * 4 + r])

    eye = (lax.broadcasted_iota(jnp.int32, (256, 256), 0)
           == lax.broadcasted_iota(jnp.int32, (256, 256), 1)).astype(f32).astype(bf16)

    def turn(src, ps):
        def step(t, _):
            cols = pl.ds(al(t * 256, 256), 256)
            v = lax.dot_general(eye, src[:, cols], NT, preferred_element_type=f32).astype(bf16)
            for p in ps:
                for j in range(16):
                    y, x, z, c = t // 2, t % 2 * 2 + j // 8, j // 2 % 4, j % 2
                    wy, wx, wz = ORDER[p]
                    k = y * wy + x * wx + z * wz
                    row = 16 * (k // 32 * 32 + c * 16 + k % 32)
                    lt[p, pl.ds(al(row), 16), :] = v[j * 16:(j + 1) * 16]
            return 0
        lax.fori_loop(0, 8, step, 0)

    def scale():
        def step(i, _):
            s = pl.ds(al(i * 32, 32), 32)
            g = gain[s, 0:1]
            og[s, :] = (g * og[s, :].astype(f32)).astype(bf16)
            return 0
        lax.fori_loop(0, 18, step, 0)

    def nn(h, p):
        w = jnp.concatenate([wt[h * 3 + p, pl.ds(place(p, d), 16), :] for d in range(128)], axis=0)
        lhs = og if p == 2 else tok
        acc[p] = jnp.dot(lhs[...], w, preferred_element_type=f32)

    def act(h):
        def step(i, _):
            s = pl.ds(al(i * 64, 64), 64)
            g, u, a = acc[0, s, :], acc[1, s, :], acc[2, s, :]
            sg = jax.nn.sigmoid(g)
            si = g * sg
            gr[h * 3 + 2, s, :] = (si * u).astype(bf16)
            gr[h * 3, s, :] = (a * u * sg * (1.0 + g * (1.0 - sg))).astype(bf16)
            gr[h * 3 + 1, s, :] = (a * si).astype(bf16)
            return 0
        lax.fori_loop(0, 9, step, 0)

    def rs_dot(h, r):
        def fn(q):
            hq = h * 3 + q
            row = (coord(q) + r) % 4 * 512
            mine = lt[q, pl.ds(al(row + core * 256, 256), 256), :]
            theirs = lt[q, pl.ds(al(row + 256 - core * 256, 256), 256), :]
            v = jnp.dot(jnp.concatenate([theirs, mine], axis=0), gr[hq], preferred_element_type=f32)
            sd[q * 4 + r] = v[0:256].astype(bf16)
            rcopy(sd.at[q * 4 + r], rd.at[hq * 4 + r], dS.at[hq * 4 + r], dR.at[hq * 4 + r], sib)
            part[q * 4 + r] = v[256:512]
        each(fn)

    def sd_done(h):
        def fn(q):
            for r in range(4):
                got(sd.at[q * 4 + r], dS.at[(h * 3 + q) * 4 + r])
        each(fn)

    def rs_far(h):
        def fn(q):
            hq = h * 3 + q
            far = rd.at[hq * 4 + 2]
            got(far, dR.at[hq * 4 + 2])
            far[...] = (part[q * 4 + 2] + far[...].astype(f32)).astype(bf16)
            lo, hi = pl.ds(0, 128), pl.ds(128, 128)
            rcopy(far.at[lo], cr.at[hq * 3, lo], cS.at[hq * 4], cR.at[hq * 4], dev(q, 1))
            rcopy(far.at[hi], cr.at[hq * 3, hi], cS.at[hq * 4 + 1], cR.at[hq * 4 + 1], dev(q, 3))
        each(fn)

    def rs_near(h, r):
        i, thru, rest = (0, pl.ds(0, 128), pl.ds(128, 128)) if r == 1 else (1, pl.ds(128, 128), pl.ds(0, 128))

        def fn(q):
            hq = h * 3 + q
            near = rd.at[hq * 4 + r]
            got(near, dR.at[hq * 4 + r])
            near[rest, :] = (part[q * 4 + r, rest, :] + near[rest, :].astype(f32)).astype(bf16)
            got(cr.at[hq * 3, thru], cR.at[hq * 4 + i])
            near[thru, :] = (part[q * 4 + r, thru, :] + near[thru, :].astype(f32)
                             + cr[hq * 3, thru, :].astype(f32)).astype(bf16)
            rcopy(near, cr.at[hq * 3 + 1 + i], cS.at[hq * 4 + 2 + i], cR.at[hq * 4 + 2 + i], dev(q, r))
        each(fn)

    def rs_b(h):
        def fn(q):
            hq = h * 3 + q
            mid = rd.at[hq * 4]
            got(mid, dR.at[hq * 4])
            got(cr.at[hq * 3 + 1], cR.at[hq * 4 + 2])
            got(cr.at[hq * 3 + 2], cR.at[hq * 4 + 3])
            v = (part[q * 4] + mid[...].astype(f32)
                 + cr[hq * 3 + 1].astype(f32) + cr[hq * 3 + 2].astype(f32))
            part[q * 4] = v
            mid[...] = v.astype(bf16)
            b = ax(q)[1]
            kb = coord(b)
            for r in (1, 2, 3):
                rcopy(mid.at[pl.ds(al((kb + r) % 4 * 64, 64), 64)], br.at[hq, pl.ds((r - 1) * 64, 64)],
                      bS.at[hq], bR.at[hq], dev(b, r))
        each(fn)

    def rs_a(h):
        def fn(q):
            hq = h * 3 + q
            _, b, a = ax(q)
            row = al(coord(b) * 64, 64)
            mine = pl.ds(row, 64)
            got(br.at[hq], bR.at[hq])
            v = part[q * 4, mine, :]
            for r in range(3):
                v = v + br[hq, pl.ds(r * 64, 64), :].astype(f32)
            part[q * 4, mine, :] = v
            rd[hq * 4, mine, :] = v.astype(bf16)
            for r in (1, 2, 3):
                rcopy(rd.at[hq * 4, pl.ds(al(row + (coord(a) + r) % 4 * 16), 16)], ar.at[hq, pl.ds((r - 1) * 16, 16)],
                      aS.at[hq], aR.at[hq], dev(a, r))
        each(fn)

    def rs_end(h):
        for q, out in enumerate((out_g, out_u, out_d)):
            hq = h * 3 + q
            _, b, a = ax(q)
            got(ar.at[hq], aR.at[hq])
            v = part[q * 4, pl.ds(al(coord(b) * 64 + coord(a) * 16), 16), :]
            for r in range(3):
                v = v + ar[hq, pl.ds(r * 16, 16), :].astype(f32)
            out[:, h * F:(h + 1) * F] = v

    def rows_out(t0, t1):
        def step(t, _):
            def nat(hp, p):
                wy, wx, wz = ORDER[p]
                ps = []
                for j in range(32):
                    x, z, c = j // 8, j // 2 % 4, j % 2
                    k = t * wy + x * wx + z * wz
                    ps.append(wt[hp, pl.ds(al(16 * (k // 32 * 32 + c * 16 + k % 32)), 16), :])
                return jnp.concatenate(ps, axis=0)
            cols = pl.ds(al(t * 512, 512), 512)
            m = g = None
            for h in range(H):
                d = lax.dot_general(gr[h * 3 + 2], nat(h * 3 + 2, 2), NT, preferred_element_type=f32)
                m = d if m is None else m + d
            mixed[:, cols] = (gain[:, 0:1] * m).astype(bf16)
            for h in range(H):
                for p in (0, 1):
                    d = lax.dot_general(gr[h * 3 + p], nat(h * 3 + p, p), NT, preferred_element_type=f32)
                    g = d if g is None else g + d
            tgrad[:, cols] = g.astype(bf16)
            return 0
        lax.fori_loop(t0, t1, step, 0)

    ag_a(0)
    ag_a(1)
    big[0].wait()
    ag_b(0)
    turn(tok, (0, 1))
    ag_c(0)
    ag_b(1)
    big[1].wait()
    big[2].wait()
    scale()
    turn(og, (2,))
    ag_c(1)
    ag_f(0)
    ag_g(0)
    for p in range(3):
        ag_wait(0, p)
        nn(0, p)
        if p == 1:
            ag_f(1)
    act(0)
    rs_dot(0, 2)
    ag_g(1)
    rs_far(0)
    rs_dot(0, 1)
    rs_dot(0, 3)
    rs_near(0, 1)
    rs_near(0, 3)
    rs_dot(0, 0)
    for p in range(3):
        ag_wait(1, p)
        nn(1, p)
    act(1)
    sd_done(0)
    rs_dot(1, 2)
    rs_b(0)
    rs_far(1)
    rs_dot(1, 1)
    rs_dot(1, 3)
    rs_a(0)
    rs_near(1, 1)
    rs_near(1, 3)
    rs_end(0)
    rs_dot(1, 0)
    rows_out(0, 2)
    rs_b(1)
    rows_out(2, 3)
    rs_a(1)
    rows_out(3, 4)
    rs_end(1)

    sd_done(1)
    for hp in range(3 * H):
        got(wt.at[hp, pl.ds(0, 2032)], ss.at[hp])
        got(rd.at[hp, pl.ds(0, 128)], cS.at[hp * 4])
        got(rd.at[hp, pl.ds(0, 128)], cS.at[hp * 4 + 1])
        got(rd.at[hp], cS.at[hp * 4 + 2])
        got(rd.at[hp], cS.at[hp * 4 + 3])
        got(br.at[hp], bS.at[hp])
        got(ar.at[hp], aS.at[hp])


def body(tokens, route_gate, cotangent, row_count, w_gate, w_up, w_down):
    rows, width = tokens.shape
    ff = w_gate.shape[1]
    F = ff // H
    live = jnp.arange(rows, dtype=jnp.int32) < row_count[0]
    gain = jnp.where(live, route_gate, jnp.zeros_like(route_gate)).astype(f32)
    gain = jnp.broadcast_to(gain[:, None], (rows, 128))
    anyspace = pl.BlockSpec(memory_space=pl.ANY)
    vmem = pl.BlockSpec(memory_space=pltpu.VMEM)
    dma = pltpu.SemaphoreType.DMA
    n = 3 * H
    return pl.pallas_call(
        kernel,
        out_shape=(
            jax.ShapeDtypeStruct((rows, width), bf16),
            jax.ShapeDtypeStruct((rows, width), bf16),
            jax.ShapeDtypeStruct((16, ff), f32),
            jax.ShapeDtypeStruct((16, ff), f32),
            jax.ShapeDtypeStruct((16, ff), f32),
        ),
        in_specs=[anyspace] * 6,
        out_specs=[vmem] * 5,
        scratch_shapes=[
            pltpu.VMEM((rows, width), bf16),
            pltpu.VMEM((rows, width), bf16),
            pltpu.VMEM((rows, 128), f32),
            pltpu.VMEM((n, width, F), bf16),
            pltpu.VMEM((3, width, rows), bf16),
            pltpu.VMEM((3, rows, F), f32),
            pltpu.VMEM((n, rows, F), bf16),
            pltpu.VMEM((12, 256, F), f32),
            pltpu.VMEM((12, 256, F), bf16),
            pltpu.VMEM((n * 4, 256, F), bf16),
            pltpu.VMEM((n * 3, 256, F), bf16),
            pltpu.VMEM((n, 192, F), bf16),
            pltpu.VMEM((n, 48, F), bf16),
            dma((9,)), dma((n,)), dma((n,)), dma((n,)), dma((n * 4,)), dma((n * 2,)), dma((n * 4,)),
            dma((n * 4,)), dma((n * 4,)), dma((n * 4,)), dma((n * 4,)),
            dma((n,)), dma((n,)), dma((n,)), dma((n,)),
        ],
        compiler_params=pltpu.CompilerParams(
            collective_id=0, has_side_effects=True, vmem_limit_bytes=64 * 1024 * 1024 - 65536),
        cost_estimate=pl.CostEstimate(
            flops=18 * rows * width * ff, bytes_accessed=8 * rows * width, transcendentals=rows * ff),
    )(tokens, cotangent, gain, w_gate, w_up, w_down)


def solution(mesh):
    row, vec = P("dp", None), P("dp")
    return jax.shard_map(
        body,
        mesh=mesh,
        in_specs=(row, vec, row, vec, row, row, row),
        out_specs=(row,) * 5,
        check_vma=False,
    )
```

```python
import functools

import jax
import jax.numpy as jnp
from jax import lax
from jax.experimental import pallas as pl
from jax.experimental.pallas import tpu as pltpu
from jax.sharding import PartitionSpec as P

bf16 = jnp.bfloat16
f32 = jnp.float32
H = 4
NT = (((1,), (1,)), ((), ()))
ORDER = ((32, 4, 1), (1, 32, 4), (4, 1, 32))


def place(p, d):
    y, x, z, core = d // 32, d // 8 % 4, d // 2 % 4, d % 2
    k = y * ORDER[p][0] + x * ORDER[p][1] + z * ORDER[p][2]
    return 16 * (k // 32 * 32 + core * 16 + k % 32)


def al(v, n=16):
    return pl.multiple_of(v, n)


def kernel(
    tok_in, cot_in, gate_in, count, wg_in, wu_in, wd_in,
    mixed, tgrad, out_g, out_u, out_d,
    tok, og, gain, wt, lt, acc, gr, part, sd, rd, cr, br, ar,
    loc, ss, ra, rb, rc, rf, rdg, dS, dR, cS, cR, bS, bR, aS, aR,
):
    F = wt.shape[2]
    me = lax.axis_index("dp")
    core = me % 2
    sib = me + 1 - 2 * core

    pos = (me // 32, me // 8 % 4, me // 2 % 4)
    peer = [[me + ((pos[p] + r) % 4 - pos[p]) * st for r in range(4)] for p, st in enumerate((32, 8, 2))]

    def coord(p):
        return pos[p]

    def dev(p, r):
        return peer[p][r]

    def ax(p):
        return p, (p + 1) % 3, (p + 2) % 3

    def rcopy(src, dst, ssem, rsem, to):
        c = pltpu.make_async_remote_copy(
            src_ref=src, dst_ref=dst, send_sem=ssem, recv_sem=rsem,
            device_id=(to,), device_id_type=pl.DeviceIdType.MESH)
        c.start()

    def got(ref, sem):
        pltpu.make_async_copy(ref, ref, sem).wait()

    def each(fn):
        for p in range(3):
            fn(p)

    def loop(fn):
        def step(p, _):
            fn(p)
            return 0
        lax.fori_loop(0, 3, step, 0)

    own = [pos[0] * wy + pos[1] * wx + pos[2] * wz for wy, wx, wz in ORDER]
    own = [al(16 * (k // 32 * 32 + core * 16 + k % 32)) for k in own]
    cps = []
    for h in range(H):
        for p, w in enumerate((wg_in, wu_in, wd_in)):
            cps.append(pltpu.make_async_copy(
                w.at[:, pl.ds(h * F, F)], wt.at[h * 3 + p, pl.ds(own[p], 16)], loc.at[h * 3 + p]))
    big = [pltpu.make_async_copy(tok_in, tok, loc.at[3 * H]),
           pltpu.make_async_copy(cot_in, og, loc.at[3 * H + 1])]
    for c in cps + big:
        c.start()

    bar = pltpu.get_barrier_semaphore()
    for p in range(3):
        for r in (1, 2, 3):
            pl.semaphore_signal(bar, inc=1, device_id=(dev(p, r),), device_id_type=pl.DeviceIdType.MESH)
    pl.semaphore_signal(bar, inc=1, device_id=(sib,), device_id_type=pl.DeviceIdType.MESH)
    pl.semaphore_wait(bar, 10)
    for c in cps:
        c.wait()

    def base(p):
        sl, mi, fa = ax(p)
        return coord(sl), coord(mi), coord(fa)

    def ag_a(h):
        def fn(p):
            kc, kb, ka = base(p)
            hp = h * 3 + p
            blk = wt.at[hp, pl.ds(al(kc * 512 + core * 256 + kb * 64 + ka * 16), 16)]
            for r in (1, 2, 3):
                rcopy(blk, blk, ss.at[hp], ra.at[hp], dev(ax(p)[2], r))
        each(fn)

    def line(p, hp, kb):
        return wt.at[hp, pl.ds(al(coord(p) * 512 + core * 256 + kb * 64, 64), 64)]

    def send_line(p, hp, kb):
        ref = line(p, hp, kb)
        half = kb // 2
        rcopy(ref, ref, ss.at[hp], rc.at[hp * 4 + half], dev(p, 1))
        rcopy(ref, ref, ss.at[hp], rc.at[hp * 4 + 2 + half], dev(p, 3))

    def ag_b(h):
        def fn(p):
            hp = h * 3 + p
            kb = coord(ax(p)[1])
            got(wt.at[hp, pl.ds(0, 48)], ra.at[hp])
            ref = line(p, hp, kb)
            for r in (1, 2, 3):
                rcopy(ref, ref, ss.at[hp], rb.at[hp], dev(ax(p)[1], r))
            send_line(p, hp, kb)
        each(fn)

    def plane(hp, kc):
        return wt.at[hp, pl.ds(al(kc * 512 + core * 256, 256), 256)]

    def to_sib(p, hp, r):
        ref = plane(hp, (coord(p) + r) % 4)
        rcopy(ref, ref, ss.at[hp], rdg.at[hp * 4 + r], sib)

    def ag_c(h):
        def fn(p):
            hp = h * 3 + p
            kb = coord(ax(p)[1])
            got(wt.at[hp, pl.ds(0, 192)], rb.at[hp])
            for j in (1, 2, 3):
                send_line(p, hp, (kb + j) % 4)
            to_sib(p, hp, 0)
        each(fn)

    def ag_f(h):
        def fn(p):
            hp = h * 3 + p
            low = wt.at[hp, pl.ds(0, 128)]
            got(low, rc.at[hp * 4])
            src = wt.at[hp, pl.ds(al((coord(p) + 3) % 4 * 512 + core * 256, 256), 128)]
            rcopy(src, src, ss.at[hp], rf.at[hp * 2], dev(p, 1))
            got(low, rc.at[hp * 4 + 3])
            src = wt.at[hp, pl.ds(al((coord(p) + 1) % 4 * 512 + core * 256 + 128, 128), 128)]
            rcopy(src, src, ss.at[hp], rf.at[hp * 2 + 1], dev(p, 3))
            got(low, rc.at[hp * 4 + 1])
            to_sib(p, hp, 3)
            got(low, rc.at[hp * 4 + 2])
            to_sib(p, hp, 1)
        each(fn)

    def ag_g(h):
        def fn(p):
            hp = h * 3 + p
            got(wt.at[hp, pl.ds(0, 128)], rf.at[hp * 2])
            got(wt.at[hp, pl.ds(0, 128)], rf.at[hp * 2 + 1])
            to_sib(p, hp, 2)
        each(fn)

    eye = (lax.broadcasted_iota(jnp.int32, (256, 256), 0)
           == lax.broadcasted_iota(jnp.int32, (256, 256), 1)).astype(f32).astype(bf16)

    def turn(src, ps):
        def step(t, _):
            cols = pl.ds(al(t * 256, 256), 256)
            v = lax.dot_general(eye, src[:, cols], NT, preferred_element_type=f32).astype(bf16)
            for p in ps:
                for j in range(16):
                    y, x, z, c = t // 2, t % 2 * 2 + j // 8, j // 2 % 4, j % 2
                    wy, wx, wz = ORDER[p]
                    k = y * wy + x * wx + z * wz
                    row = 16 * (k // 32 * 32 + c * 16 + k % 32)
                    lt[p, pl.ds(al(row), 16), :] = v[j * 16:(j + 1) * 16]
            return 0
        lax.fori_loop(0, 8, step, 0)

    def scale():
        n = tok.shape[0]
        g = gate_in[...].astype(f32)
        g = jnp.where(lax.broadcasted_iota(jnp.int32, (1, n), 1) < count[0], g, 0.0)
        diag = lax.broadcasted_iota(jnp.int32, (n, n), 0) == lax.broadcasted_iota(jnp.int32, (n, n), 1)
        gain[...] = jnp.dot(jnp.where(diag, jnp.broadcast_to(g, (n, n)), 0.0).astype(bf16),
                            jnp.ones((n, 128), bf16), preferred_element_type=f32)

        def step(i, _):
            s = pl.ds(al(i * 32, 32), 32)
            og[s, :] = (gain[s, 0:1] * og[s, :].astype(f32)).astype(bf16)
            return 0
        lax.fori_loop(0, n // 32, step, 0)

    def nat(h, p, ds):
        return jnp.concatenate([wt[h * 3 + p, pl.ds(place(p, d), 16), :] for d in ds], axis=0)

    def nn(h, k):
        for p in ((0, 1), (2,))[k]:
            for r in range(4):
                got(plane(h * 3 + p, r), rdg.at[(h * 3 + p) * 4 + r])
        if k == 0:
            w = jnp.concatenate([nat(h, 0, range(128)), nat(h, 1, range(128))], axis=1)
            v = jnp.dot(tok[...], w, preferred_element_type=f32)
            acc[0] = v[:, :F]
            acc[1] = v[:, F:]
        else:
            acc[2] = jnp.dot(og[...], nat(h, 2, range(128)), preferred_element_type=f32)

    def act(h):
        def step(i, _):
            s = pl.ds(al(i * 64, 64), 64)
            g, u, a = acc[0, s, :], acc[1, s, :], acc[2, s, :]
            sg = jax.nn.sigmoid(g)
            si = g * sg
            gr[h * 3 + 2, s, :] = (si * u).astype(bf16)
            gr[h * 3, s, :] = (a * u * sg * (1.0 + g * (1.0 - sg))).astype(bf16)
            gr[h * 3 + 1, s, :] = (a * si).astype(bf16)
            return 0
        lax.fori_loop(0, 9, step, 0)

    def slot(h, q, r):
        return ((h % 2) * 3 + q) * 4 + r

    def held(h, q, r):
        return part.at[h * 3 + q if r == 0 else 3 * H + (h % 2) * 9 + q * 3 + r - 1]

    def sd_done(h, rs):
        for q in range(3):
            for r in rs:
                got(sd.at[slot(h, q, r)], dS.at[(h * 3 + q) * 4 + r])

    def rs_dot(h, k):
        rs = ((2, 1), (3, 0))[k]
        if h >= 2:
            sd_done(h - 2, rs)

        def fn(q):
            hq = h * 3 + q
            kc = pos[0] + q * (pos[1] - pos[0]) + q * (q - 1) // 2 * (pos[2] - 2 * pos[1] + pos[0])
            rows = []
            for r in rs:
                row = (kc + r) % 4 * 512
                rows.append(lt[q, pl.ds(al(row + 256 - core * 256, 256), 256), :])
                rows.append(lt[q, pl.ds(al(row + core * 256, 256), 256), :])
            v = jnp.dot(jnp.concatenate(rows, axis=0), gr[hq], preferred_element_type=f32)
            for i, r in enumerate(rs):
                at = slot(h, q, r)
                sd[at] = v[i * 512:i * 512 + 256].astype(bf16)
                rcopy(sd.at[at], rd.at[hq * 4 + r], dS.at[hq * 4 + r], dR.at[hq * 4 + r], sib)
                held(h, q, r)[...] = v[i * 512 + 256:(i + 1) * 512]
        loop(fn)

    def rs_far(h):
        def fn(q):
            hq = h * 3 + q
            far = rd.at[hq * 4 + 2]
            got(far, dR.at[hq * 4 + 2])
            far[...] = (held(h, q, 2)[...] + far[...].astype(f32)).astype(bf16)
            lo, hi = pl.ds(0, 128), pl.ds(128, 128)
            rcopy(far.at[lo], cr.at[hq * 3, lo], cS.at[hq * 6], cR.at[hq * 6], dev(q, 1))
            rcopy(far.at[hi], cr.at[hq * 3, hi], cS.at[hq * 6 + 1], cR.at[hq * 6 + 1], dev(q, 3))
        each(fn)

    def rs_near(h, r):
        i, rest = (0, pl.ds(128, 128)) if r == 1 else (1, pl.ds(0, 128))

        def fn(q):
            hq = h * 3 + q
            near = rd.at[hq * 4 + r]
            got(near, dR.at[hq * 4 + r])
            near[rest, :] = (held(h, q, r)[rest, :] + near[rest, :].astype(f32)).astype(bf16)
            rcopy(near.at[rest], cr.at[hq * 3 + 1 + i, rest], cS.at[hq * 6 + 2 + i], cR.at[hq * 6 + 2 + i], dev(q, r))
        each(fn)

    def rs_thru(h, r):
        i, thru = (0, pl.ds(0, 128)) if r == 1 else (1, pl.ds(128, 128))

        def fn(q):
            hq = h * 3 + q
            near = rd.at[hq * 4 + r]
            got(cr.at[hq * 3, thru], cR.at[hq * 6 + i])
            near[thru, :] = (held(h, q, r)[thru, :] + near[thru, :].astype(f32)
                             + cr[hq * 3, thru, :].astype(f32)).astype(bf16)
            rcopy(near.at[thru], cr.at[hq * 3 + 1 + i, thru], cS.at[hq * 6 + 4 + i], cR.at[hq * 6 + 4 + i], dev(q, r))
        each(fn)

    def rs_b(h):
        def fn(q):
            hq = h * 3 + q
            mid = rd.at[hq * 4]
            got(mid, dR.at[hq * 4])
            for i in range(4):
                got(cr.at[hq * 3 + 1, pl.ds(0, 128)], cR.at[hq * 6 + 2 + i])
            v = (held(h, q, 0)[...] + mid[...].astype(f32)
                 + cr[hq * 3 + 1].astype(f32) + cr[hq * 3 + 2].astype(f32))
            held(h, q, 0)[...] = v
            mid[...] = v.astype(bf16)
            b = ax(q)[1]
            kb = coord(b)
            for r in (1, 2, 3):
                rcopy(mid.at[pl.ds(al((kb + r) % 4 * 64, 64), 64)], br.at[hq, pl.ds((r - 1) * 64, 64)],
                      bS.at[hq], bR.at[hq], dev(b, r))
        each(fn)

    def rs_a(h):
        def fn(q):
            hq = h * 3 + q
            _, b, a = ax(q)
            row = al(coord(b) * 64, 64)
            mine = pl.ds(row, 64)
            got(br.at[hq], bR.at[hq])
            v = held(h, q, 0)[mine, :]
            for r in range(3):
                v = v + br[hq, pl.ds(r * 64, 64), :].astype(f32)
            held(h, q, 0)[mine, :] = v
            rd[hq * 4, mine, :] = v.astype(bf16)
            for r in (1, 2, 3):
                rcopy(rd.at[hq * 4, pl.ds(al(row + (coord(a) + r) % 4 * 16), 16)], ar.at[hq, pl.ds((r - 1) * 16, 16)],
                      aS.at[hq], aR.at[hq], dev(a, r))
        each(fn)

    def rs_end(h):
        for q, out in enumerate((out_g, out_u, out_d)):
            hq = h * 3 + q
            _, b, a = ax(q)
            got(ar.at[hq], aR.at[hq])
            v = held(h, q, 0)[pl.ds(al(coord(b) * 64 + coord(a) * 16), 16), :]
            for r in range(3):
                v = v + ar[hq, pl.ds(r * 16, 16), :].astype(f32)
            out[:, h * F:(h + 1) * F] = v

    def rows_out(t):
        ds = range(t * 32, t * 32 + 32)
        cols = pl.ds(t * 512, 512)

        def wide(p):
            return (jnp.concatenate([gr[h * 3 + p] for h in range(H)], axis=1),
                    jnp.concatenate([nat(h, p, ds) for h in range(H)], axis=1))
        mixed[:, cols] = (gain[:, 0:1] * lax.dot_general(*wide(2), NT, preferred_element_type=f32)).astype(bf16)
        tgrad[:, cols] = (lax.dot_general(*wide(0), NT, preferred_element_type=f32)
                          + lax.dot_general(*wide(1), NT, preferred_element_type=f32)).astype(bf16)

    ag_a(0)
    ag_a(1)
    ag_a(2)
    ag_a(3)
    big[0].wait()
    turn(tok, (0, 1))
    ag_b(0)
    big[1].wait()
    scale()
    ag_b(1)
    turn(og, (2,))
    ag_c(0)
    ag_c(1)
    ag_f(0)
    ag_b(2)
    ag_f(1)
    ag_b(3)
    ag_g(0)
    nn(0, 0)
    ag_c(2)
    nn(0, 1)
    act(0)
    rs_dot(0, 0)
    ag_g(1)
    ag_c(3)
    rs_dot(0, 1)
    nn(1, 1)
    ag_f(2)
    rs_near(0, 3)
    rs_near(0, 1)
    nn(1, 0)
    act(1)
    rs_dot(1, 0)
    rs_far(0)
    ag_f(3)
    ag_g(2)
    rs_far(1)
    rs_dot(1, 1)
    nn(2, 0)
    rs_thru(0, 1)
    rs_near(1, 3)
    nn(2, 1)
    rs_near(1, 1)
    ag_g(3)
    act(2)
    rs_thru(0, 3)
    rs_dot(2, 0)
    nn(3, 1)
    rs_far(2)
    rs_near(2, 1)
    rs_thru(1, 3)
    rs_dot(2, 1)
    nn(3, 0)
    rs_near(2, 3)
    rs_thru(1, 1)
    rs_thru(2, 3)
    act(3)
    rs_thru(2, 1)
    rs_dot(3, 0)
    rs_far(3)
    rs_b(0)
    rs_dot(3, 1)
    rs_near(3, 1)
    rs_near(3, 3)
    rs_thru(3, 3)
    rs_thru(3, 1)
    rs_b(1)
    rs_b(2)
    rs_a(0)
    rows_out(0)
    rs_b(3)
    rows_out(1)
    rs_a(1)
    rows_out(2)
    rs_a(2)
    rs_a(3)
    rs_end(1)
    rows_out(3)
    rs_end(2)
    rs_end(0)
    rs_end(3)

    for h in (H - 2, H - 1):
        sd_done(h, range(4))
    for hp in range(3 * H):
        got(wt.at[hp, pl.ds(0, 2032)], ss.at[hp])
        for i in range(6):
            got(rd.at[hp, pl.ds(0, 128)], cS.at[hp * 6 + i])
        got(br.at[hp], bS.at[hp])
        got(ar.at[hp], aS.at[hp])


def deliver(*refs):
    n = len(refs) // 2
    cps = [pltpu.make_async_copy(refs[i], refs[n + i], refs[2 * n].at[i]) for i in range(n)]
    for c in cps:
        c.start()
    for c in cps:
        c.wait()


def body(tokens, route_gate, cotangent, row_count, w_gate, w_up, w_down):
    rows, width = tokens.shape
    ff = w_gate.shape[1]
    F = ff // H
    anyspace = pl.BlockSpec(memory_space=pl.ANY)
    vmem = pl.BlockSpec(memory_space=pltpu.VMEM)
    dma = pltpu.SemaphoreType.DMA
    n = 3 * H
    parts = pl.pallas_call(
        kernel,
        out_shape=(
            pltpu.VMEM((rows, width), bf16),
            pltpu.VMEM((rows, width), bf16),
            pltpu.VMEM((16, ff), f32),
            pltpu.VMEM((16, ff), f32),
            pltpu.VMEM((16, ff), f32),
        ),
        in_specs=[anyspace, anyspace, vmem, pl.BlockSpec(memory_space=pltpu.SMEM), anyspace, anyspace, anyspace],
        out_specs=[vmem] * 5,
        scratch_shapes=[
            pltpu.VMEM((rows, width), bf16),
            pltpu.VMEM((rows, width), bf16),
            pltpu.VMEM((rows, 128), f32),
            pltpu.VMEM((n, width, F), bf16),
            pltpu.VMEM((3, width, rows), bf16),
            pltpu.VMEM((3, rows, F), f32),
            pltpu.VMEM((n, rows, F), bf16),
            pltpu.VMEM((n + 18, 256, F), f32),
            pltpu.VMEM((24, 256, F), bf16),
            pltpu.VMEM((n * 4, 256, F), bf16),
            pltpu.VMEM((n * 3, 256, F), bf16),
            pltpu.VMEM((n, 192, F), bf16),
            pltpu.VMEM((n, 48, F), bf16),
            dma((n + 2,)), dma((n,)), dma((n,)), dma((n,)), dma((n * 4,)), dma((n * 2,)), dma((n * 4,)),
            dma((n * 4,)), dma((n * 4,)), dma((n * 6,)), dma((n * 6,)),
            dma((n,)), dma((n,)), dma((n,)), dma((n,)),
        ],
        compiler_params=pltpu.CompilerParams(
            collective_id=0, has_side_effects=True, vmem_limit_bytes=57 * 1024 * 1024),
        cost_estimate=pl.CostEstimate(
            flops=18 * rows * width * ff, bytes_accessed=8 * rows * width, transcendentals=rows * ff),
    )(tokens, cotangent, route_gate[None, :], row_count, w_gate, w_up, w_down)
    return pl.pallas_call(
        deliver,
        out_shape=tuple(jax.ShapeDtypeStruct(v.shape, v.dtype) for v in parts),
        in_specs=[vmem] * 5,
        out_specs=[anyspace] * 5,
        scratch_shapes=[dma((5,))],
        compiler_params=pltpu.CompilerParams(vmem_limit_bytes=1024 * 1024),
    )(*parts)


def solution(mesh):
    row, vec = P("dp", None), P("dp")
    return jax.shard_map(
        body,
        mesh=mesh,
        in_specs=(row, vec, row, vec, row, row, row),
        out_specs=(row,) * 5,
        check_vma=False,
    )
```

```python
import functools

import jax
import jax.numpy as jnp
from jax import lax
from jax.experimental import pallas as pl
from jax.experimental.pallas import tpu as pltpu
from jax.sharding import PartitionSpec as P

bf16 = jnp.bfloat16
f32 = jnp.float32
H = 4
NT = (((1,), (1,)), ((), ()))
FAR_GATHER = ()
FAR_REDUCE = ()
PLANE_GATHER = (0, 1,)
PLANE_REDUCE = (3,)
ORDER = ((32, 4, 1), (1, 32, 4), (4, 1, 32))


def place(p, d):
    y, x, z, core = d // 32, d // 8 % 4, d // 2 % 4, d % 2
    k = y * ORDER[p][0] + x * ORDER[p][1] + z * ORDER[p][2]
    return 16 * (k // 32 * 32 + core * 16 + k % 32)


def al(v, n=16):
    return pl.multiple_of(v, n)


def kernel(
    tok_in, cot_in, gate_in, count, wg_in, wu_in, wd_in,
    mixed, tgrad, out_g, out_u, out_d,
    tok, og, gain, wt, lt, acc, gr, part, sd, rd, cr, br, ar,
    loc, ss, ra, rb, rc, rf, rdg, dS, dR, cS, cR, bS, bR, aS, aR,
):
    F = wt.shape[2]
    me = lax.axis_index("dp")
    core = me % 2
    sib = me + 1 - 2 * core

    pos = (me // 32, me // 8 % 4, me // 2 % 4)
    peer = [[me + ((pos[p] + r) % 4 - pos[p]) * st for r in range(4)] for p, st in enumerate((32, 8, 2))]

    def across(p, rb, ra):
        _, b, a = ax(p)
        return peer[b][rb] + peer[a][ra] - me

    def coord(p):
        return pos[p]

    def dev(p, r):
        return peer[p][r]

    def ax(p):
        return p, (p + 1) % 3, (p + 2) % 3

    def rcopy(src, dst, ssem, rsem, to):
        c = pltpu.make_async_remote_copy(
            src_ref=src, dst_ref=dst, send_sem=ssem, recv_sem=rsem,
            device_id=(to,), device_id_type=pl.DeviceIdType.MESH)
        c.start()

    def got(ref, sem):
        pltpu.make_async_copy(ref, ref, sem).wait()

    def each(fn):
        for p in range(3):
            fn(p)

    own = [pos[0] * wy + pos[1] * wx + pos[2] * wz for wy, wx, wz in ORDER]
    own = [al(16 * (k // 32 * 32 + core * 16 + k % 32)) for k in own]
    cps = []
    for h in range(H):
        for p, w in enumerate((wg_in, wu_in, wd_in)):
            cps.append(pltpu.make_async_copy(
                w.at[:, pl.ds(h * F, F)], wt.at[h * 3 + p, pl.ds(own[p], 16)], loc.at[h * 3 + p]))
    big = [pltpu.make_async_copy(tok_in, tok, loc.at[3 * H]),
           pltpu.make_async_copy(cot_in, og, loc.at[3 * H + 1])]
    for c in cps + big:
        c.start()

    bar = pltpu.get_barrier_semaphore()
    meet = [dev(p, r) for p in range(3) for r in (1, 2, 3)] + [sib]
    if PLANE_GATHER or PLANE_REDUCE:
        meet += [across(p, rb, ra) for p in range(3) for rb in (1, 2, 3) for ra in (1, 2, 3)]
    for to in meet:
        pl.semaphore_signal(bar, inc=1, device_id=(to,), device_id_type=pl.DeviceIdType.MESH)
    pl.semaphore_wait(bar, len(meet))
    for c in cps:
        c.wait()

    def base(p):
        sl, mi, fa = ax(p)
        return coord(sl), coord(mi), coord(fa)

    def ag_a(h):
        def fn(p):
            kc, kb, ka = base(p)
            hp = h * 3 + p
            blk = wt.at[hp, pl.ds(al(kc * 512 + core * 256 + kb * 64 + ka * 16), 16)]
            if h in PLANE_GATHER:
                for i in range(1, 16):
                    rcopy(blk, blk, ss.at[hp], rb.at[hp], across(p, i // 4, i % 4))
                return
            for r in (1, 2, 3):
                rcopy(blk, blk, ss.at[hp], ra.at[hp], dev(ax(p)[2], r))
        each(fn)

    def line(p, hp, kb):
        return wt.at[hp, pl.ds(al(coord(p) * 512 + core * 256 + kb * 64, 64), 64)]

    def send_line(p, hp, kb):
        ref = line(p, hp, kb)
        half = kb // 2
        rcopy(ref, ref, ss.at[hp], rc.at[hp * 4 + half], dev(p, 1))
        rcopy(ref, ref, ss.at[hp], rc.at[hp * 4 + 2 + half], dev(p, 3))
        if hp // 3 in FAR_GATHER:
            rcopy(ref, ref, ss.at[hp], rf.at[hp * 2 + half], dev(p, 2))

    def ag_b(h):
        def fn(p):
            hp = h * 3 + p
            kb = coord(ax(p)[1])
            if h in PLANE_GATHER:
                return
            got(wt.at[hp, pl.ds(0, 48)], ra.at[hp])
            ref = line(p, hp, kb)
            for r in (1, 2, 3):
                rcopy(ref, ref, ss.at[hp], rb.at[hp], dev(ax(p)[1], r))
            send_line(p, hp, kb)
        each(fn)

    def plane(hp, kc):
        return wt.at[hp, pl.ds(al(kc * 512 + core * 256, 256), 256)]

    def to_sib(p, hp, r):
        ref = plane(hp, (coord(p) + r) % 4)
        rcopy(ref, ref, ss.at[hp], rdg.at[hp * 4 + r], sib)

    def ag_c(h):
        def fn(p):
            hp = h * 3 + p
            kb = coord(ax(p)[1])
            got(wt.at[hp, pl.ds(0, 240 if h in PLANE_GATHER else 192)], rb.at[hp])
            for j in range(0 if h in PLANE_GATHER else 1, 4):
                send_line(p, hp, (kb + j) % 4)
            to_sib(p, hp, 0)
        each(fn)

    def ag_f(h):
        def fn(p):
            hp = h * 3 + p
            low = wt.at[hp, pl.ds(0, 128)]
            got(low, rc.at[hp * 4])
            if h not in FAR_GATHER:
                src = wt.at[hp, pl.ds(al((coord(p) + 3) % 4 * 512 + core * 256, 256), 128)]
                rcopy(src, src, ss.at[hp], rf.at[hp * 2], dev(p, 1))
            got(low, rc.at[hp * 4 + 3])
            if h not in FAR_GATHER:
                src = wt.at[hp, pl.ds(al((coord(p) + 1) % 4 * 512 + core * 256 + 128, 128), 128)]
                rcopy(src, src, ss.at[hp], rf.at[hp * 2 + 1], dev(p, 3))
            got(low, rc.at[hp * 4 + 1])
            to_sib(p, hp, 3)
            got(low, rc.at[hp * 4 + 2])
            to_sib(p, hp, 1)
        each(fn)

    def ag_g(h):
        def fn(p):
            hp = h * 3 + p
            got(wt.at[hp, pl.ds(0, 128)], rf.at[hp * 2])
            got(wt.at[hp, pl.ds(0, 128)], rf.at[hp * 2 + 1])
            to_sib(p, hp, 2)
        each(fn)

    def turn(src, ps):
        def step(t, _):
            cols = pl.ds(al(t * 256, 256), 256)
            v = src[:, cols].T
            for p in ps:
                for j in range(16):
                    y, x, z, c = t // 2, t % 2 * 2 + j // 8, j // 2 % 4, j % 2
                    wy, wx, wz = ORDER[p]
                    k = y * wy + x * wx + z * wz
                    row = 16 * (k // 32 * 32 + c * 16 + k % 32)
                    lt[p, pl.ds(al(row), 16), :] = v[j * 16:(j + 1) * 16]
            return 0
        lax.fori_loop(0, 8, step, 0)

    def scale():
        n = tok.shape[0]
        g = gate_in[...].astype(f32).reshape(1, n)
        g = jnp.where(lax.broadcasted_iota(jnp.int32, (1, n), 1) < count[0], g, 0.0)
        diag = lax.broadcasted_iota(jnp.int32, (n, n), 0) == lax.broadcasted_iota(jnp.int32, (n, n), 1)
        gain[...] = jnp.dot(jnp.where(diag, jnp.broadcast_to(g, (n, n)), 0.0).astype(bf16),
                            jnp.ones((n, 128), bf16), preferred_element_type=f32)

        def step(i, _):
            s = pl.ds(al(i * 32, 32), 32)
            og[s, :] = (gain[s, 0:1] * og[s, :].astype(f32)).astype(bf16)
            return 0
        lax.fori_loop(0, n // 32, step, 0)

    def nat(h, p, ds):
        return jnp.concatenate([wt[h * 3 + p, pl.ds(place(p, d), 16), :] for d in ds], axis=0)

    def nn(h, k):
        for p in ((0, 1), (2,))[k]:
            for r in range(4):
                got(plane(h * 3 + p, r), rdg.at[(h * 3 + p) * 4 + r])
        if k == 0:
            w = jnp.concatenate([nat(h, 0, range(128)), nat(h, 1, range(128))], axis=1)
            v = jnp.dot(tok[...], w, preferred_element_type=f32)
            acc[0] = v[:, :F]
            acc[1] = v[:, F:]
        else:
            acc[2] = jnp.dot(og[...], nat(h, 2, range(128)), preferred_element_type=f32)

    def act(h):
        def step(i, _):
            s = pl.ds(al(i * 64, 64), 64)
            g, u, a = acc[0, s, :], acc[1, s, :], acc[2, s, :]
            sg = jax.nn.sigmoid(g)
            si = g * sg
            gr[h * 3 + 2, s, :] = (si * u).astype(bf16)
            gr[h * 3, s, :] = (a * u * sg * (1.0 + g * (1.0 - sg))).astype(bf16)
            gr[h * 3 + 1, s, :] = (a * si).astype(bf16)
            return 0
        lax.fori_loop(0, 9, step, 0)

    def slot(h, q, r):
        return ((h % 2) * 3 + q) * 4 + r

    def held(h, q, r):
        return part.at[h * 3 + q if r == 0 else 3 * H + (h % 2) * 9 + q * 3 + r - 1]

    def sd_done(h, rs):
        for q in range(3):
            for r in rs:
                got(sd.at[slot(h, q, r)], dS.at[(h * 3 + q) * 4 + r])

    def rs_dot(h, k):
        rs = ((2, 1), (3, 0))[k]
        if h >= 2:
            sd_done(h - 2, rs)

        for q in range(3):
            rows = []
            for r in rs:
                row = (pos[q] + r) % 4 * 512
                rows.append(lt[q, pl.ds(al(row + 256 - core * 256, 256), 256), :])
                rows.append(lt[q, pl.ds(al(row + core * 256, 256), 256), :])
            v = jnp.dot(jnp.concatenate(rows, axis=0), gr[h * 3 + q], preferred_element_type=f32)
            for i, r in enumerate(rs):
                sd[slot(h, q, r)] = v[i * 512:i * 512 + 256].astype(bf16)
                held(h, q, r)[...] = v[i * 512 + 256:(i + 1) * 512]
        for q in range(3):
            hq = h * 3 + q
            for r in rs:
                rcopy(sd.at[slot(h, q, r)], rd.at[hq * 4 + r], dS.at[hq * 4 + r], dR.at[hq * 4 + r], sib)

    def rs_far(h):
        def fn(q):
            hq = h * 3 + q
            far = rd.at[hq * 4 + 2]
            got(far, dR.at[hq * 4 + 2])
            far[...] = (held(h, q, 2)[...] + far[...].astype(f32)).astype(bf16)
            if h in FAR_REDUCE:
                rcopy(far, cr.at[hq * 3], cS.at[hq * 6], cR.at[hq * 6], dev(q, 2))
                return
            lo, hi = pl.ds(0, 128), pl.ds(128, 128)
            rcopy(far.at[lo], cr.at[hq * 3, lo], cS.at[hq * 6], cR.at[hq * 6], dev(q, 1))
            rcopy(far.at[hi], cr.at[hq * 3, hi], cS.at[hq * 6 + 1], cR.at[hq * 6 + 1], dev(q, 3))
        each(fn)

    def rs_near(h, r):
        i, rest = (0, pl.ds(128, 128)) if r == 1 else (1, pl.ds(0, 128))
        if h in FAR_REDUCE:
            rest = pl.ds(0, 256)

        def fn(q):
            hq = h * 3 + q
            near = rd.at[hq * 4 + r]
            got(near, dR.at[hq * 4 + r])
            near[rest, :] = (held(h, q, r)[rest, :] + near[rest, :].astype(f32)).astype(bf16)
            rcopy(near.at[rest], cr.at[hq * 3 + 1 + i, rest], cS.at[hq * 6 + 2 + i], cR.at[hq * 6 + 2 + i], dev(q, r))
        each(fn)

    def rs_thru(h, r):
        i, thru = (0, pl.ds(0, 128)) if r == 1 else (1, pl.ds(128, 128))
        if h in FAR_REDUCE:
            return

        def fn(q):
            hq = h * 3 + q
            near = rd.at[hq * 4 + r]
            got(cr.at[hq * 3, thru], cR.at[hq * 6 + i])
            near[thru, :] = (held(h, q, r)[thru, :] + near[thru, :].astype(f32)
                             + cr[hq * 3, thru, :].astype(f32)).astype(bf16)
            rcopy(near.at[thru], cr.at[hq * 3 + 1 + i, thru], cS.at[hq * 6 + 4 + i], cR.at[hq * 6 + 4 + i], dev(q, r))
        each(fn)

    def slow_done(hq, sem, halves, first):
        whole, half = cr.at[hq * 3 + 1], cr.at[hq * 3 + 1, pl.ds(0, 128)]
        if halves:
            for i in range(0 if first else 2, 6):
                got(half, sem.at[hq * 6 + i])
        else:
            for i in (0, 2, 3):
                got(whole, sem.at[hq * 6 + i])

    def rs_b(h):
        def fn(q):
            hq = h * 3 + q
            mid = rd.at[hq * 4]
            got(mid, dR.at[hq * 4])
            slow_done(hq, cR, h not in FAR_REDUCE, False)
            v = (held(h, q, 0)[...] + mid[...].astype(f32)
                 + cr[hq * 3 + 1].astype(f32) + cr[hq * 3 + 2].astype(f32))
            if h in FAR_REDUCE:
                v = v + cr[hq * 3].astype(f32)
            held(h, q, 0)[...] = v
            mid[...] = v.astype(bf16)
            _, b, a = ax(q)
            kb = coord(b)
            if h in PLANE_REDUCE:
                for i in range(1, 16):
                    src = mid.at[pl.ds(al((kb + i // 4) % 4 * 64 + (coord(a) + i % 4) % 4 * 16), 16)]
                    if i < 13:
                        rcopy(src, br.at[hq, pl.ds(i * 16 - 16, 16)], bS.at[hq], bR.at[hq], across(q, i // 4, i % 4))
                    else:
                        rcopy(src, ar.at[hq, pl.ds(i * 16 - 208, 16)], aS.at[hq], aR.at[hq], across(q, i // 4, i % 4))
                return
            for r in (1, 2, 3):
                rcopy(mid.at[pl.ds(al((kb + r) % 4 * 64, 64), 64)], br.at[hq, pl.ds((r - 1) * 64, 64)],
                      bS.at[hq], bR.at[hq], dev(b, r))
        each(fn)

    def rs_a(h):
        def fn(q):
            hq = h * 3 + q
            _, b, a = ax(q)
            row = al(coord(b) * 64, 64)
            mine = pl.ds(row, 64)
            if h in PLANE_REDUCE:
                return
            got(br.at[hq], bR.at[hq])
            v = held(h, q, 0)[mine, :]
            for r in range(3):
                v = v + br[hq, pl.ds(r * 64, 64), :].astype(f32)
            held(h, q, 0)[mine, :] = v
            rd[hq * 4, mine, :] = v.astype(bf16)
            for r in (1, 2, 3):
                rcopy(rd.at[hq * 4, pl.ds(al(row + (coord(a) + r) % 4 * 16), 16)], ar.at[hq, pl.ds((r - 1) * 16, 16)],
                      aS.at[hq], aR.at[hq], dev(a, r))
        each(fn)

    def rs_end(h):
        for q, out in enumerate((out_g, out_u, out_d)):
            hq = h * 3 + q
            _, b, a = ax(q)
            got(ar.at[hq], aR.at[hq])
            v = held(h, q, 0)[pl.ds(al(coord(b) * 64 + coord(a) * 16), 16), :]
            for r in range(3):
                v = v + ar[hq, pl.ds(r * 16, 16), :].astype(f32)
            if h in PLANE_REDUCE:
                got(br.at[hq], bR.at[hq])
                for r in range(12):
                    v = v + br[hq, pl.ds(r * 16, 16), :].astype(f32)
            out[:, h * F:(h + 1) * F] = v

    def rows_out(t):
        ds = range(t * 32, t * 32 + 32)
        cols = pl.ds(t * 512, 512)

        def wide(p):
            return (jnp.concatenate([gr[h * 3 + p] for h in range(H)], axis=1),
                    jnp.concatenate([nat(h, p, ds) for h in range(H)], axis=1))
        mixed[:, cols] = (gain[:, 0:1] * lax.dot_general(*wide(2), NT, preferred_element_type=f32)).astype(bf16)
        tgrad[:, cols] = (lax.dot_general(*wide(0), NT, preferred_element_type=f32)
                          + lax.dot_general(*wide(1), NT, preferred_element_type=f32)).astype(bf16)

    ag_a(0)
    ag_a(1)
    ag_a(2)
    ag_a(3)
    big[1].wait()
    scale()
    big[0].wait()
    turn(tok, (0, 1))
    ag_c(0)
    ag_c(1)
    turn(og, (2,))
    ag_f(0)
    ag_b(2)
    ag_f(1)
    ag_b(3)
    ag_g(0)
    nn(0, 0)
    nn(0, 1)
    act(0)
    ag_c(2)
    ag_g(1)
    rs_dot(0, 1)
    ag_c(3)
    nn(1, 1)
    rs_dot(0, 0)
    ag_f(2)
    nn(1, 0)
    act(1)
    ag_f(3)
    rs_dot(1, 0)
    rs_far(0)
    ag_g(2)
    rs_near(0, 1)
    rs_dot(1, 1)
    rs_near(0, 3)
    rs_far(1)
    nn(2, 1)
    rs_near(1, 1)
    nn(2, 0)
    act(2)
    rs_near(1, 3)
    ag_g(3)
    rs_thru(0, 3)
    rs_thru(0, 1)
    rs_dot(2, 0)
    nn(3, 0)
    rs_far(2)
    rs_dot(2, 1)
    rs_thru(1, 3)
    rs_thru(1, 1)
    nn(3, 1)
    act(3)
    rs_near(2, 1)
    rs_near(2, 3)
    rs_dot(3, 0)
    rs_thru(2, 3)
    rs_thru(2, 1)
    rs_dot(3, 1)
    rs_far(3)
    rs_near(3, 1)
    rs_b(1)
    rs_near(3, 3)
    rows_out(0)
    rs_thru(3, 1)
    rs_thru(3, 3)
    rs_b(2)
    rs_b(0)
    rows_out(1)
    rs_b(3)
    rows_out(2)
    rs_a(0)
    rs_a(1)
    rs_a(2)
    rows_out(3)
    rs_end(1)
    rs_end(2)
    rs_end(0)
    rs_end(3)

    for h in (H - 2, H - 1):
        sd_done(h, range(4))
    for hp in range(3 * H):
        got(wt.at[hp, pl.ds(0, 2032)], ss.at[hp])
        slow_done(hp, cS, hp // 3 not in FAR_REDUCE, True)
        got(br.at[hp], bS.at[hp])
        got(ar.at[hp], aS.at[hp])


def deliver(*refs):
    n = len(refs) // 2
    cps = [pltpu.make_async_copy(refs[i], refs[n + i], refs[2 * n].at[i]) for i in range(n)]
    for c in cps:
        c.start()
    for c in cps:
        c.wait()


def body(tokens, route_gate, cotangent, row_count, w_gate, w_up, w_down):
    rows, width = tokens.shape
    ff = w_gate.shape[1]
    F = ff // H
    anyspace = pl.BlockSpec(memory_space=pl.ANY)
    vmem = pl.BlockSpec(memory_space=pltpu.VMEM)
    dma = pltpu.SemaphoreType.DMA
    n = 3 * H
    parts = pl.pallas_call(
        kernel,
        out_shape=(
            pltpu.VMEM((rows, width), bf16),
            pltpu.VMEM((rows, width), bf16),
            pltpu.VMEM((16, ff), f32),
            pltpu.VMEM((16, ff), f32),
            pltpu.VMEM((16, ff), f32),
        ),
        in_specs=[anyspace, anyspace, vmem, pl.BlockSpec(memory_space=pltpu.SMEM), anyspace, anyspace, anyspace],
        out_specs=[vmem] * 5,
        scratch_shapes=[
            pltpu.VMEM((rows, width), bf16),
            pltpu.VMEM((rows, width), bf16),
            pltpu.VMEM((rows, 128), f32),
            pltpu.VMEM((n, width, F), bf16),
            pltpu.VMEM((3, width, rows), bf16),
            pltpu.VMEM((3, rows, F), f32),
            pltpu.VMEM((n, rows, F), bf16),
            pltpu.VMEM((n + 18, 256, F), f32),
            pltpu.VMEM((24, 256, F), bf16),
            pltpu.VMEM((n * 4, 256, F), bf16),
            pltpu.VMEM((n * 3, 256, F), bf16),
            pltpu.VMEM((n, 192, F), bf16),
            pltpu.VMEM((n, 48, F), bf16),
            dma((n + 2,)), dma((n,)), dma((n,)), dma((n,)), dma((n * 4,)), dma((n * 2,)), dma((n * 4,)),
            dma((n * 4,)), dma((n * 4,)), dma((n * 6,)), dma((n * 6,)),
            dma((n,)), dma((n,)), dma((n,)), dma((n,)),
        ],
        compiler_params=pltpu.CompilerParams(
            collective_id=0, has_side_effects=True, vmem_limit_bytes=57 * 1024 * 1024),
        cost_estimate=pl.CostEstimate(
            flops=18 * rows * width * ff, bytes_accessed=8 * rows * width, transcendentals=rows * ff),
    )(tokens, cotangent, route_gate, row_count, w_gate, w_up, w_down)
    return pl.pallas_call(
        deliver,
        out_shape=tuple(jax.ShapeDtypeStruct(v.shape, v.dtype) for v in parts),
        in_specs=[vmem] * 5,
        out_specs=[anyspace] * 5,
        scratch_shapes=[dma((5,))],
        compiler_params=pltpu.CompilerParams(vmem_limit_bytes=1024 * 1024),
    )(*parts)


def solution(mesh):
    row, vec = P("dp", None), P("dp")
    return jax.shard_map(
        body,
        mesh=mesh,
        in_specs=(row, vec, row, vec, row, row, row),
        out_specs=(row,) * 5,
        check_vma=False,
    )
```

```python
import functools

import jax
import jax.numpy as jnp
from jax import lax
from jax.experimental import pallas as pl
from jax.experimental.pallas import tpu as pltpu
from jax.sharding import PartitionSpec as P

bf16 = jnp.bfloat16
f32 = jnp.float32
H = 4
NT = (((1,), (1,)), ((), ()))
FAR_GATHER = ()
FAR_REDUCE = ()
PLANE_GATHER = (0, 1,)
PLANE_REDUCE = (3,)
ORDER = ((32, 4, 1), (1, 32, 4), (4, 1, 32))


def place(p, d):
    y, x, z, core = d // 32, d // 8 % 4, d // 2 % 4, d % 2
    k = y * ORDER[p][0] + x * ORDER[p][1] + z * ORDER[p][2]
    return 16 * (k // 32 * 32 + core * 16 + k % 32)


def al(v, n=16):
    return pl.multiple_of(v, n)


def kernel(
    tok_in, cot_in, gate_in, count, wg_in, wu_in, wd_in,
    mixed, tgrad, out_g, out_u, out_d,
    tok, og, gain, wt, lt, acc, gr, part, sd, rd, cr, br, ar,
    loc, ss, ra, rb, rc, rf, rdg, dS, dR, cS, cR, bS, bR, aS, aR,
):
    F = wt.shape[2]
    me = lax.axis_index("dp")
    core = me % 2
    sib = me + 1 - 2 * core

    pos = (me // 32, me // 8 % 4, me // 2 % 4)
    peer = [[me + ((pos[p] + r) % 4 - pos[p]) * st for r in range(4)] for p, st in enumerate((32, 8, 2))]

    def across(p, rb, ra):
        _, b, a = ax(p)
        return peer[b][rb] + peer[a][ra] - me

    def coord(p):
        return pos[p]

    def dev(p, r):
        return peer[p][r]

    def ax(p):
        return p, (p + 1) % 3, (p + 2) % 3

    def rcopy(src, dst, ssem, rsem, to):
        c = pltpu.make_async_remote_copy(
            src_ref=src, dst_ref=dst, send_sem=ssem, recv_sem=rsem,
            device_id=(to,), device_id_type=pl.DeviceIdType.MESH)
        c.start()

    def got(ref, sem):
        pltpu.make_async_copy(ref, ref, sem).wait()

    def each(fn):
        for p in range(3):
            fn(p)

    own = [pos[0] * wy + pos[1] * wx + pos[2] * wz for wy, wx, wz in ORDER]
    own = [al(16 * (k // 32 * 32 + core * 16 + k % 32)) for k in own]
    cps = []
    for h in range(H):
        for p, w in enumerate((wg_in, wu_in, wd_in)):
            cps.append(pltpu.make_async_copy(
                w.at[:, pl.ds(h * F, F)], wt.at[h * 3 + p, pl.ds(own[p], 16)], loc.at[h * 3 + p]))
    big = [pltpu.make_async_copy(tok_in, tok, loc.at[3 * H]),
           pltpu.make_async_copy(cot_in, og, loc.at[3 * H + 1])]
    for c in cps + big:
        c.start()

    bar = pltpu.get_barrier_semaphore()
    meet = [dev(p, r) for p in range(3) for r in (1, 2, 3)] + [sib]
    if PLANE_GATHER or PLANE_REDUCE:
        meet += [across(p, rb, ra) for p in range(3) for rb in (1, 2, 3) for ra in (1, 2, 3)]
    for to in meet:
        pl.semaphore_signal(bar, inc=1, device_id=(to,), device_id_type=pl.DeviceIdType.MESH)
    pl.semaphore_wait(bar, len(meet))
    for c in cps:
        c.wait()

    def base(p):
        sl, mi, fa = ax(p)
        return coord(sl), coord(mi), coord(fa)

    def ag_a(h):
        def fn(p):
            kc, kb, ka = base(p)
            hp = h * 3 + p
            blk = wt.at[hp, pl.ds(al(kc * 512 + core * 256 + kb * 64 + ka * 16), 16)]
            if h in PLANE_GATHER:
                for i in range(1, 16):
                    rcopy(blk, blk, ss.at[hp], rb.at[hp], across(p, i // 4, i % 4))
                return
            for r in (1, 2, 3):
                rcopy(blk, blk, ss.at[hp], ra.at[hp], dev(ax(p)[2], r))
        each(fn)

    def line(p, hp, kb):
        return wt.at[hp, pl.ds(al(coord(p) * 512 + core * 256 + kb * 64, 64), 64)]

    def send_line(p, hp, kb):
        ref = line(p, hp, kb)
        half = kb // 2
        rcopy(ref, ref, ss.at[hp], rc.at[hp * 4 + half], dev(p, 1))
        rcopy(ref, ref, ss.at[hp], rc.at[hp * 4 + 2 + half], dev(p, 3))
        if hp // 3 in FAR_GATHER:
            rcopy(ref, ref, ss.at[hp], rf.at[hp * 2 + half], dev(p, 2))

    def ag_b(h):
        def fn(p):
            hp = h * 3 + p
            kb = coord(ax(p)[1])
            if h in PLANE_GATHER:
                return
            got(wt.at[hp, pl.ds(0, 48)], ra.at[hp])
            ref = line(p, hp, kb)
            for r in (1, 2, 3):
                rcopy(ref, ref, ss.at[hp], rb.at[hp], dev(ax(p)[1], r))
            send_line(p, hp, kb)
        each(fn)

    def plane(hp, kc):
        return wt.at[hp, pl.ds(al(kc * 512 + core * 256, 256), 256)]

    def to_sib(p, hp, r):
        ref = plane(hp, (coord(p) + r) % 4)
        rcopy(ref, ref, ss.at[hp], rdg.at[hp * 4 + r], sib)

    def ag_c(h):
        def fn(p):
            hp = h * 3 + p
            kb = coord(ax(p)[1])
            got(wt.at[hp, pl.ds(0, 240 if h in PLANE_GATHER else 192)], rb.at[hp])
            for j in range(0 if h in PLANE_GATHER else 1, 4):
                send_line(p, hp, (kb + j) % 4)
            to_sib(p, hp, 0)
        each(fn)

    def ag_f(h):
        def fn(p):
            hp = h * 3 + p
            low = wt.at[hp, pl.ds(0, 128)]
            got(low, rc.at[hp * 4])
            if h not in FAR_GATHER:
                src = wt.at[hp, pl.ds(al((coord(p) + 3) % 4 * 512 + core * 256, 256), 128)]
                rcopy(src, src, ss.at[hp], rf.at[hp * 2], dev(p, 1))
            got(low, rc.at[hp * 4 + 3])
            if h not in FAR_GATHER:
                src = wt.at[hp, pl.ds(al((coord(p) + 1) % 4 * 512 + core * 256 + 128, 128), 128)]
                rcopy(src, src, ss.at[hp], rf.at[hp * 2 + 1], dev(p, 3))
            got(low, rc.at[hp * 4 + 1])
            to_sib(p, hp, 3)
            got(low, rc.at[hp * 4 + 2])
            to_sib(p, hp, 1)
        each(fn)

    def ag_g(h):
        def fn(p):
            hp = h * 3 + p
            got(wt.at[hp, pl.ds(0, 128)], rf.at[hp * 2])
            got(wt.at[hp, pl.ds(0, 128)], rf.at[hp * 2 + 1])
            to_sib(p, hp, 2)
        each(fn)

    def turn(src, ps):
        def step(t, _):
            cols = pl.ds(al(t * 256, 256), 256)
            v = src[:, cols].T
            for p in ps:
                for j in range(16):
                    y, x, z, c = t // 2, t % 2 * 2 + j // 8, j // 2 % 4, j % 2
                    wy, wx, wz = ORDER[p]
                    k = y * wy + x * wx + z * wz
                    row = 16 * (k // 32 * 32 + c * 16 + k % 32)
                    lt[p, pl.ds(al(row), 16), :] = v[j * 16:(j + 1) * 16]
            return 0
        lax.fori_loop(0, 8, step, 0)

    def scale():
        n = tok.shape[0]
        g = gate_in[...].astype(f32).reshape(1, n)
        g = jnp.where(lax.broadcasted_iota(jnp.int32, (1, n), 1) < count[0], g, 0.0)
        diag = lax.broadcasted_iota(jnp.int32, (n, n), 0) == lax.broadcasted_iota(jnp.int32, (n, n), 1)
        gain[...] = jnp.dot(jnp.where(diag, jnp.broadcast_to(g, (n, n)), 0.0).astype(bf16),
                            jnp.ones((n, 128), bf16), preferred_element_type=f32)

        def step(i, _):
            s = pl.ds(al(i * 32, 32), 32)
            og[s, :] = (gain[s, 0:1] * og[s, :].astype(f32)).astype(bf16)
            return 0
        lax.fori_loop(0, n // 32, step, 0)

    def nat(h, p, ds):
        return jnp.concatenate([wt[h * 3 + p, pl.ds(place(p, d), 16), :] for d in ds], axis=0)

    def nn(h, k):
        for p in ((0, 1), (2,))[k]:
            for r in range(4):
                got(plane(h * 3 + p, r), rdg.at[(h * 3 + p) * 4 + r])
        if k == 0:
            w = jnp.concatenate([nat(h, 0, range(128)), nat(h, 1, range(128))], axis=1)
            v = jnp.dot(tok[...], w, preferred_element_type=f32)
            acc[0] = v[:, :F]
            acc[1] = v[:, F:]
        else:
            acc[2] = jnp.dot(og[...], nat(h, 2, range(128)), preferred_element_type=f32)

    def act(h):
        def step(i, _):
            s = pl.ds(al(i * 64, 64), 64)
            g, u, a = acc[0, s, :], acc[1, s, :], acc[2, s, :]
            sg = jax.nn.sigmoid(g)
            si = g * sg
            gr[h * 3 + 2, s, :] = (si * u).astype(bf16)
            gr[h * 3, s, :] = (a * u * sg * (1.0 + g * (1.0 - sg))).astype(bf16)
            gr[h * 3 + 1, s, :] = (a * si).astype(bf16)
            return 0
        lax.fori_loop(0, 9, step, 0)

    def slot(h, q, r):
        return ((h % 2) * 3 + q) * 4 + r

    def held(h, q, r):
        return part.at[h * 3 + q if r == 0 else 3 * H + (h % 2) * 9 + q * 3 + r - 1]

    def sd_done(h, rs):
        for q in range(3):
            for r in rs:
                got(sd.at[slot(h, q, r)], dS.at[(h * 3 + q) * 4 + r])

    def rs_dot(h, k):
        rs = ((2, 1), (3, 0))[k]
        if h >= 2:
            sd_done(h - 2, rs)

        for q in range(3):
            rows = []
            for r in rs:
                row = (pos[q] + r) % 4 * 512
                rows.append(lt[q, pl.ds(al(row + 256 - core * 256, 256), 256), :])
                rows.append(lt[q, pl.ds(al(row + core * 256, 256), 256), :])
            v = jnp.dot(jnp.concatenate(rows, axis=0), gr[h * 3 + q], preferred_element_type=f32)
            for i, r in enumerate(rs):
                sd[slot(h, q, r)] = v[i * 512:i * 512 + 256].astype(bf16)
                held(h, q, r)[...] = v[i * 512 + 256:(i + 1) * 512]
        for q in range(3):
            hq = h * 3 + q
            for r in rs:
                rcopy(sd.at[slot(h, q, r)], rd.at[hq * 4 + r], dS.at[hq * 4 + r], dR.at[hq * 4 + r], sib)

    def rs_far(h):
        def fn(q):
            hq = h * 3 + q
            far = rd.at[hq * 4 + 2]
            got(far, dR.at[hq * 4 + 2])
            far[...] = (held(h, q, 2)[...] + far[...].astype(f32)).astype(bf16)
            if h in FAR_REDUCE:
                rcopy(far, cr.at[hq * 3], cS.at[hq * 6], cR.at[hq * 6], dev(q, 2))
                return
            lo, hi = pl.ds(0, 128), pl.ds(128, 128)
            rcopy(far.at[lo], cr.at[hq * 3, lo], cS.at[hq * 6], cR.at[hq * 6], dev(q, 1))
            rcopy(far.at[hi], cr.at[hq * 3, hi], cS.at[hq * 6 + 1], cR.at[hq * 6 + 1], dev(q, 3))
        each(fn)

    def rs_near(h, r):
        i, rest = (0, pl.ds(128, 128)) if r == 1 else (1, pl.ds(0, 128))
        if h in FAR_REDUCE:
            rest = pl.ds(0, 256)

        def fn(q):
            hq = h * 3 + q
            near = rd.at[hq * 4 + r]
            got(near, dR.at[hq * 4 + r])
            near[rest, :] = (held(h, q, r)[rest, :] + near[rest, :].astype(f32)).astype(bf16)
            rcopy(near.at[rest], cr.at[hq * 3 + 1 + i, rest], cS.at[hq * 6 + 2 + i], cR.at[hq * 6 + 2 + i], dev(q, r))
        each(fn)

    def rs_thru(h, r):
        i, thru = (0, pl.ds(0, 128)) if r == 1 else (1, pl.ds(128, 128))
        if h in FAR_REDUCE:
            return

        def fn(q):
            hq = h * 3 + q
            near = rd.at[hq * 4 + r]
            got(cr.at[hq * 3, thru], cR.at[hq * 6 + i])
            near[thru, :] = (held(h, q, r)[thru, :] + near[thru, :].astype(f32)
                             + cr[hq * 3, thru, :].astype(f32)).astype(bf16)
            rcopy(near.at[thru], cr.at[hq * 3 + 1 + i, thru], cS.at[hq * 6 + 4 + i], cR.at[hq * 6 + 4 + i], dev(q, r))
        each(fn)

    def slow_done(hq, sem, halves, first):
        whole, half = cr.at[hq * 3 + 1], cr.at[hq * 3 + 1, pl.ds(0, 128)]
        if halves:
            for i in range(0 if first else 2, 6):
                got(half, sem.at[hq * 6 + i])
        else:
            for i in (0, 2, 3):
                got(whole, sem.at[hq * 6 + i])

    def rs_b(h):
        def fn(q):
            hq = h * 3 + q
            mid = rd.at[hq * 4]
            got(mid, dR.at[hq * 4])
            slow_done(hq, cR, h not in FAR_REDUCE, False)
            v = (held(h, q, 0)[...] + mid[...].astype(f32)
                 + cr[hq * 3 + 1].astype(f32) + cr[hq * 3 + 2].astype(f32))
            if h in FAR_REDUCE:
                v = v + cr[hq * 3].astype(f32)
            held(h, q, 0)[...] = v
            mid[...] = v.astype(bf16)
            _, b, a = ax(q)
            kb = coord(b)
            if h in PLANE_REDUCE:
                for i in range(1, 16):
                    src = mid.at[pl.ds(al((kb + i // 4) % 4 * 64 + (coord(a) + i % 4) % 4 * 16), 16)]
                    if i < 13:
                        rcopy(src, br.at[hq, pl.ds(i * 16 - 16, 16)], bS.at[hq], bR.at[hq], across(q, i // 4, i % 4))
                    else:
                        rcopy(src, ar.at[hq, pl.ds(i * 16 - 208, 16)], aS.at[hq], aR.at[hq], across(q, i // 4, i % 4))
                return
            for r in (1, 2, 3):
                rcopy(mid.at[pl.ds(al((kb + r) % 4 * 64, 64), 64)], br.at[hq, pl.ds((r - 1) * 64, 64)],
                      bS.at[hq], bR.at[hq], dev(b, r))
        each(fn)

    def rs_a(h):
        def fn(q):
            hq = h * 3 + q
            _, b, a = ax(q)
            row = al(coord(b) * 64, 64)
            mine = pl.ds(row, 64)
            if h in PLANE_REDUCE:
                return
            got(br.at[hq], bR.at[hq])
            v = held(h, q, 0)[mine, :]
            for r in range(3):
                v = v + br[hq, pl.ds(r * 64, 64), :].astype(f32)
            held(h, q, 0)[mine, :] = v
            rd[hq * 4, mine, :] = v.astype(bf16)
            for r in (1, 2, 3):
                rcopy(rd.at[hq * 4, pl.ds(al(row + (coord(a) + r) % 4 * 16), 16)], ar.at[hq, pl.ds((r - 1) * 16, 16)],
                      aS.at[hq], aR.at[hq], dev(a, r))
        each(fn)

    def rs_end(h):
        for q, out in enumerate((out_g, out_u, out_d)):
            hq = h * 3 + q
            _, b, a = ax(q)
            got(ar.at[hq], aR.at[hq])
            v = held(h, q, 0)[pl.ds(al(coord(b) * 64 + coord(a) * 16), 16), :]
            for r in range(3):
                v = v + ar[hq, pl.ds(r * 16, 16), :].astype(f32)
            if h in PLANE_REDUCE:
                got(br.at[hq], bR.at[hq])
                for r in range(12):
                    v = v + br[hq, pl.ds(r * 16, 16), :].astype(f32)
            out[:, h * F:(h + 1) * F] = v

    def rows_out(t):
        ds = range(t * 32, t * 32 + 32)
        cols = pl.ds(t * 512, 512)

        def wide(p):
            return (jnp.concatenate([gr[h * 3 + p] for h in range(H)], axis=1),
                    jnp.concatenate([nat(h, p, ds) for h in range(H)], axis=1))
        mixed[:, cols] = (gain[:, 0:1] * lax.dot_general(*wide(2), NT, preferred_element_type=f32)).astype(bf16)
        tgrad[:, cols] = (lax.dot_general(*wide(0), NT, preferred_element_type=f32)
                          + lax.dot_general(*wide(1), NT, preferred_element_type=f32)).astype(bf16)

    ag_a(0)
    ag_a(1)
    ag_a(2)
    ag_a(3)
    big[1].wait()
    scale()
    big[0].wait()
    turn(tok, (0, 1))
    turn(og, (2,))
    ag_c(0)
    ag_c(1)
    ag_f(0)
    ag_b(2)
    ag_f(1)
    ag_b(3)
    ag_g(0)
    nn(0, 0)
    nn(0, 1)
    act(0)
    ag_c(2)
    ag_g(1)
    rs_dot(0, 0)
    nn(1, 0)
    rs_far(0)
    nn(1, 1)
    act(1)
    ag_f(2)
    rs_dot(0, 1)
    ag_c(3)
    rs_dot(1, 1)
    rs_near(0, 1)
    rs_thru(0, 1)
    rs_near(0, 3)
    rs_thru(0, 3)
    ag_g(2)
    rs_dot(1, 0)
    nn(2, 1)
    ag_f(3)
    nn(2, 0)
    rs_far(1)
    act(2)
    rs_near(1, 3)
    rs_dot(2, 0)
    rs_near(1, 1)
    ag_g(3)
    rs_dot(2, 1)
    rs_far(2)
    rs_b(0)
    rs_thru(1, 1)
    nn(3, 1)
    rs_near(2, 3)
    rs_thru(1, 3)
    rs_near(2, 1)
    nn(3, 0)
    act(3)
    rs_dot(3, 0)
    rs_thru(2, 3)
    rs_thru(2, 1)
    rs_dot(3, 1)
    rs_far(3)
    rs_near(3, 1)
    rs_b(1)
    rs_near(3, 3)
    rows_out(0)
    rs_thru(3, 1)
    rs_thru(3, 3)
    rs_b(2)
    rows_out(1)
    rs_a(0)
    rs_a(1)
    rs_b(3)
    rows_out(2)
    rs_a(2)
    rows_out(3)
    rs_end(1)
    rs_end(0)
    rs_end(2)
    rs_end(3)

    for h in (H - 2, H - 1):
        sd_done(h, range(4))
    for hp in range(3 * H):
        got(wt.at[hp, pl.ds(0, 2032)], ss.at[hp])
        slow_done(hp, cS, hp // 3 not in FAR_REDUCE, True)
        got(br.at[hp], bS.at[hp])
        got(ar.at[hp], aS.at[hp])


def deliver(*refs):
    n = len(refs) // 2
    cps = [pltpu.make_async_copy(refs[i], refs[n + i], refs[2 * n].at[i]) for i in range(n)]
    for c in cps:
        c.start()
    for c in cps:
        c.wait()


def body(tokens, route_gate, cotangent, row_count, w_gate, w_up, w_down):
    rows, width = tokens.shape
    ff = w_gate.shape[1]
    F = ff // H
    anyspace = pl.BlockSpec(memory_space=pl.ANY)
    vmem = pl.BlockSpec(memory_space=pltpu.VMEM)
    dma = pltpu.SemaphoreType.DMA
    n = 3 * H
    parts = pl.pallas_call(
        kernel,
        out_shape=(
            pltpu.VMEM((rows, width), bf16),
            pltpu.VMEM((rows, width), bf16),
            pltpu.VMEM((16, ff), f32),
            pltpu.VMEM((16, ff), f32),
            pltpu.VMEM((16, ff), f32),
        ),
        in_specs=[anyspace, anyspace, vmem, pl.BlockSpec(memory_space=pltpu.SMEM), anyspace, anyspace, anyspace],
        out_specs=[vmem] * 5,
        scratch_shapes=[
            pltpu.VMEM((rows, width), bf16),
            pltpu.VMEM((rows, width), bf16),
            pltpu.VMEM((rows, 128), f32),
            pltpu.VMEM((n, width, F), bf16),
            pltpu.VMEM((3, width, rows), bf16),
            pltpu.VMEM((3, rows, F), f32),
            pltpu.VMEM((n, rows, F), bf16),
            pltpu.VMEM((n + 18, 256, F), f32),
            pltpu.VMEM((24, 256, F), bf16),
            pltpu.VMEM((n * 4, 256, F), bf16),
            pltpu.VMEM((n * 3, 256, F), bf16),
            pltpu.VMEM((n, 192, F), bf16),
            pltpu.VMEM((n, 48, F), bf16),
            dma((n + 2,)), dma((n,)), dma((n,)), dma((n,)), dma((n * 4,)), dma((n * 2,)), dma((n * 4,)),
            dma((n * 4,)), dma((n * 4,)), dma((n * 6,)), dma((n * 6,)),
            dma((n,)), dma((n,)), dma((n,)), dma((n,)),
        ],
        compiler_params=pltpu.CompilerParams(
            collective_id=0, has_side_effects=True, vmem_limit_bytes=57 * 1024 * 1024),
        cost_estimate=pl.CostEstimate(
            flops=18 * rows * width * ff, bytes_accessed=8 * rows * width, transcendentals=rows * ff),
    )(tokens, cotangent, route_gate, row_count, w_gate, w_up, w_down)
    return pl.pallas_call(
        deliver,
        out_shape=tuple(jax.ShapeDtypeStruct(v.shape, v.dtype) for v in parts),
        in_specs=[vmem] * 5,
        out_specs=[anyspace] * 5,
        scratch_shapes=[dma((5,))],
        compiler_params=pltpu.CompilerParams(vmem_limit_bytes=1024 * 1024),
    )(*parts)


def solution(mesh):
    row, vec = P("dp", None), P("dp")
    return jax.shard_map(
        body,
        mesh=mesh,
        in_specs=(row, vec, row, vec, row, row, row),
        out_specs=(row,) * 5,
        check_vma=False,
    )
```
